32 devices in a mesh: src: 8 (over z, x), row: 4 (over y, core).
Axes of the slice: x: 2, y: 2, z: 4, core: 2. Of those that a mesh axis runs over, the one named last changes fastest.
Arguments:
- right_side: float32 [2, 8192, 2048], P(None, 'row', 'src'), may hold values from -6 to 6
- pivot_inverse: float32 [2, 2, 512, 512], P(None, None, 'src')
- ancestor_panel: float32 [2, 2, 4096, 512], P(None, None, ('row', 'src')), may hold values from -0.1875 to 0.1875
- ancestors: int32 [2, 4096], P(None, 'row'), may hold values from -1 to 2047, as said below
- pivot_block: int32 [2], replicated, may hold values from 0 to 15, as said below
Outputs:
- forward: float32 [2, 8192, 2048], P(None, 'row', 'src')
The draws below stay inside these ranges and needn't reach their ends.
Inputs may be any that keep to these rules, and one draw needn't show every extreme that they name: pivot_block holds 2 distinct blocks of 512 rows; one of them is always the last block. `ancestors`: for supernode k and row device r, slots r * 1024 to r * 1024 + 1023 hold distinct rising local rows of that device followed by -1 in the remaining slots; they never touch the pivot rows of supernodes 0 to k, and for k below 1 they include every pivot row of supernode k + 1 that lies on that device; for each supernode some row device fills all 1024 slots.
All inputs are finite; a program needn't handle non-finite values.
Results may differ from the reference program's by a relative error of at most 0.0001.
Values sent between devices are 32-bit elements; how exact they have to be, the bound alone decides.
A program may use at most 128 MiB of HBM per device.

```python
import jax
import jax.numpy as jnp
from jax import lax

P_SIZE = 512
ROWS = 8192
AD = 1024
NODES = 2
R_LOC = 2048
COLS = 2048
N_ROW = 4


def chosen_blocks(key):
    last_block = ROWS // P_SIZE - 1
    others = jax.random.permutation(jax.random.fold_in(key, 7), last_block)[:NODES - 1].astype(jnp.int32)
    picked = jnp.concatenate([others, jnp.full((1,), last_block, jnp.int32)])
    order = jax.random.permutation(jax.random.fold_in(key, 8), NODES)
    return picked[order].astype(jnp.int32)


def draw_pivot_block(key, part):
    return chosen_blocks(key)


def device_slots(key, supernode, device, blocks):
    local_rows = jnp.arange(R_LOC, dtype=jnp.int32)
    row_block = (device * R_LOC + local_rows) // P_SIZE
    excluded = jnp.zeros((R_LOC,), bool)
    for earlier in range(supernode + 1):
        excluded = excluded | (row_block == blocks[earlier])
    if supernode + 1 < NODES:
        forced = row_block == blocks[supernode + 1]
        full_device = blocks[supernode + 1] // (R_LOC // P_SIZE)
    else:
        forced = jnp.zeros((R_LOC,), bool)
        full_device = (blocks[supernode] // (R_LOC // P_SIZE) + 1) % N_ROW
    noise_bits = jax.random.randint(jax.random.fold_in(key, 1), (R_LOC,), 0, 2 ** 16)
    scores = jnp.where(forced, local_rows - R_LOC, jnp.where(excluded, 2 ** 30 + local_rows, noise_bits * R_LOC + local_rows))
    ordering = jnp.argsort(scores, stable=True)[:AD].astype(jnp.int32)
    allowed = R_LOC - jnp.sum(excluded.astype(jnp.int32))
    drawn_count = jax.random.randint(jax.random.fold_in(key, 2), (), AD // 4, AD + 1)
    count_live = jnp.where(device == full_device, AD, jnp.minimum(drawn_count, allowed))
    slots = jnp.arange(AD, dtype=jnp.int32)
    keyed = jnp.sort(jnp.where(slots < count_live, ordering, R_LOC + slots))
    return jnp.where(keyed < R_LOC, keyed, -1).astype(jnp.int32)


def draw_ancestors(key, part):
    blocks = chosen_blocks(key)
    result = []
    for supernode in range(NODES):
        node_key = jax.random.fold_in(key, 100 + supernode)
        devices = jnp.arange(N_ROW, dtype=jnp.int32)
        filled = jax.vmap(lambda device: device_slots(jax.random.fold_in(node_key, device), supernode, device, blocks))(devices)
        result.append(filled.reshape(N_ROW * AD))
    return jnp.stack(result).astype(jnp.int32)


def draw_pivot_inverse(key, part):
    first_key, second_key, third_key = jax.random.split(jax.random.fold_in(key, 11), 3)
    lines = jnp.arange(P_SIZE)
    below = (lines[:, None] > lines[None, :]).astype(jnp.float32)
    entries = jax.random.normal(first_key, (NODES, 2, P_SIZE, P_SIZE), jnp.float32) * 0.7 / P_SIZE ** 0.5
    diag_real = jax.random.uniform(second_key, (NODES, P_SIZE), jnp.float32, 0.8, 1.2)
    diag_imag = jax.random.uniform(third_key, (NODES, P_SIZE), jnp.float32, -0.4, 0.4)
    eye = jnp.eye(P_SIZE, dtype=jnp.float32)
    real_part = entries[:, 0] * below + diag_real[:, :, None] * eye
    imag_part = entries[:, 1] * below + diag_imag[:, :, None] * eye
    return jnp.stack([real_part, imag_part], axis=1).astype(jnp.float32)


def level_of(own_key, extent, cuts, smallest, largest):
    level, own = 1.0, jax.random.fold_in(own_key, 6)
    for dim, parts in cuts:
        draws = jnp.exp(jax.random.uniform(jax.random.fold_in(own, dim), (parts,), jnp.float32, smallest / len(cuts), largest / len(cuts)))
        level = level * jnp.repeat(draws, extent[dim] // parts).reshape([-1 if axis == dim else 1 for axis in range(len(extent))])
    return level


def normal_values(stream_key, extent, width, bound, cuts=(), held_as=jnp.bfloat16):
    values = width * jax.random.normal(stream_key, extent, jnp.float32)
    if cuts:
        values = values * level_of(stream_key, extent, cuts, -0.22, 0.18)
    return jnp.clip(values, -bound, bound).astype(held_as)


def setup_inputs(seed: int = 0) -> dict:
    arg_keys = jax.random.split(jax.random.key(seed), 6)
    return {
        "right_side": normal_values(arg_keys[0], (2, ROWS, COLS), 1.0, 6.0, ((1, 4), (2, 8)), jnp.float32),
        "pivot_inverse": draw_pivot_inverse(jax.random.fold_in(arg_keys[5], 71), 0),
        "ancestor_panel": normal_values(arg_keys[2], (NODES, 2, N_ROW * AD, P_SIZE), (2 * P_SIZE) ** -0.5, 0.1875, ((2, 32),), jnp.float32),
        "ancestors": draw_ancestors(jax.random.fold_in(arg_keys[5], 71), 0),
        "pivot_block": draw_pivot_block(jax.random.fold_in(arg_keys[5], 71), 0),
    }


def complex_product(factor, operand):
    hint = lax.Precision.HIGHEST
    real_part = jnp.dot(factor[0], operand[0], precision=hint, preferred_element_type=jnp.float32) - jnp.dot(factor[1], operand[1], precision=hint, preferred_element_type=jnp.float32)
    imag_part = jnp.dot(factor[0], operand[1], precision=hint, preferred_element_type=jnp.float32) + jnp.dot(factor[1], operand[0], precision=hint, preferred_element_type=jnp.float32)
    return jnp.stack([real_part, imag_part])


def reference(right_side, pivot_inverse, ancestor_panel, ancestors, pivot_block):
    front_rows = right_side
    slots = jnp.arange(N_ROW * AD, dtype=jnp.int32)
    for supernode in range(NODES):
        offset = (pivot_block[supernode] * P_SIZE).astype(jnp.int32)
        pivot_part = lax.dynamic_slice_in_dim(front_rows, offset, P_SIZE, 1)
        solved = complex_product(pivot_inverse[supernode], pivot_part)
        front_rows = lax.dynamic_update_slice_in_dim(front_rows, solved, offset, 1)
        update = complex_product(ancestor_panel[supernode], solved)
        live_slots = ancestors[supernode] >= 0
        target = jnp.where(live_slots, (slots // AD) * R_LOC + ancestors[supernode], 0).astype(jnp.int32)
        front_rows = front_rows.at[:, target, :].add(-jnp.where(live_slots[None, :, None], update, 0.0))
    return front_rows
```

```python
import functools

import jax
import jax.numpy as jnp
from jax import lax
from jax.experimental import pallas as pl
from jax.experimental.pallas import tpu as pltpu
from jax.sharding import PartitionSpec as P

MESH = pl.DeviceIdType.MESH
F32, BF16 = jnp.float32, jnp.bfloat16
TILE = 256


def halves(value):
    high = value.astype(BF16)
    return high, (value - high.astype(F32)).astype(BF16)


def mm(a, b):
    return jnp.dot(a, b, preferred_element_type=F32)


def mm3(a, b_high, b_low):
    high, low = halves(a)
    return mm(high, b_high) + (mm(high, b_low) + mm(low, b_high))


def kernel(n_src, n_row, front_ref, inverse_ref, panel_ref, slots_ref, block_ref, out_ref,
           pan, inv, cand, core_in, chip_sum, row_in, sol, w_high, w_low, u_high, u_low,
           local_sem, hop_send, hop_recv, inv_send, inv_recv, piv_send, piv_recv):
    nodes, _, shard, depth = panel_ref.shape
    inv_rows = inverse_ref.shape[2]
    quarter = depth // n_row
    half = front_ref.shape[2] // 2
    per_device = front_ref.shape[1] // depth
    slots = slots_ref.shape[1]
    nz, ny = n_src // 2, n_row // 2

    src, row = lax.axis_index("src"), lax.axis_index("row")
    z, x = src // 2, src % 2
    y, core = row // 2, row % 2
    up = {"src": src + 2, "row": row}
    down = {"src": src - 2, "row": row}
    across = {"src": z * 2 + (1 - x), "row": row}
    mate = {"src": src, "row": y * 2 + (1 - core)}
    far = [{"src": src, "row": (y + d) % ny * 2 + core} for d in range(1, ny)]

    def place(unit, index):
        if unit == 0:
            rows = pl.ds(pl.multiple_of(index * inv_rows, 8), inv_rows)
            return inv.at[:, :, row, rows, :]
        rows = pl.ds(pl.multiple_of(index * shard, 8), shard)
        return pan.at[unit - 1, :, rows, :]

    own = [pltpu.make_async_copy(
        inverse_ref.at[:, :, :, pl.ds(pl.multiple_of(row * quarter, 128), quarter)],
        place(0, src), local_sem.at[0])]
    own += [pltpu.make_async_copy(panel_ref.at[k], place(k + 1, src), local_sem.at[k + 1])
            for k in range(nodes)]
    for copy in own:
        copy.start()

    barrier = pltpu.get_barrier_semaphore()

    def greet(device):
        pl.semaphore_signal(barrier, inc=1, device_id=device, device_id_type=MESH)

    @pl.when(z + 1 < nz)
    def _():
        greet(up)

    @pl.when(z > 0)
    def _():
        greet(down)

    for device in [across, mate] + far:
        greet(device)

    ends = jnp.where(z + 1 < nz, 1, 0) + jnp.where(z > 0, 1, 0)
    pl.semaphore_wait(barrier, 2 + len(far) + ends)

    def hop(unit, jz, jx, way, device):
        index = jz * 2 + jx
        ref = place(unit, index)
        return pltpu.make_async_remote_copy(
            src_ref=ref, dst_ref=ref, send_sem=hop_send.at[unit, way, jz],
            recv_sem=hop_recv.at[unit, index], device_id=device, device_id_type=MESH)

    def go_up(unit, jz):
        @pl.when(z + 1 < nz)
        def _():
            hop(unit, jz, x, 0, up).start()

    def go_down(unit, jz):
        @pl.when(z > 0)
        def _():
            hop(unit, jz, x, 1, down).start()

    def go_across(unit, jz):
        hop(unit, jz, x, 2, across).start()

    def own_sends(unit):
        own[unit].wait()
        go_up(unit, z)
        go_down(unit, z)
        go_across(unit, z)

    def step(unit, t):
        below, above = z - t, z + t

        @pl.when(below >= 0)
        def _():
            hop(unit, below, x, 2, across).wait_recv()
            go_up(unit, below)
            go_across(unit, below)

        @pl.when(above < nz)
        def _():
            hop(unit, above, x, 2, across).wait_recv()
            go_down(unit, above)
            go_across(unit, above)

    def steps(unit, first, last):
        @pl.loop(first, last)
        def _(t):
            step(unit, t)

    def across_wait(unit):
        @pl.loop(0, nz)
        def _(j):
            hop(unit, j, 1 - x, 2, across).wait_recv()

    def sends_wait(unit):
        @pl.loop(0, nz)
        def _(j):
            @pl.when((j <= z) & (z + 1 < nz))
            def _():
                hop(unit, j, x, 0, up).wait_send()

            @pl.when((j >= z) & (z > 0))
            def _():
                hop(unit, j, x, 1, down).wait_send()

            hop(unit, j, x, 2, across).wait_send()

    def inv_copy(node, owner_y, owner_core, way, device):
        owner = owner_y * 2 + owner_core
        ref = inv.at[node, :, owner]
        return pltpu.make_async_remote_copy(
            src_ref=ref, dst_ref=ref, send_sem=inv_send.at[node, way],
            recv_sem=inv_recv.at[node, owner], device_id=device, device_id_type=MESH)

    def inv_start(node):
        for d, device in enumerate(far):
            inv_copy(node, y, core, ny + d, device).start()
        inv_copy(node, y, core, 0, mate).start()

    def inv_relay(node):
        for d in range(1, ny):
            other = (y + d) % ny
            inv_copy(node, other, core, 0, mate).wait_recv()
            inv_copy(node, other, core, d, mate).start()

    def inv_finish(node):
        for d in range(ny):
            inv_copy(node, (y + d) % ny, 1 - core, 0, mate).wait_recv()

    def inv_sends_wait(node):
        for d, device in enumerate(far):
            inv_copy(node, y, core, ny + d, device).wait_send()
        for d in range(ny):
            inv_copy(node, (y + d) % ny, core, d, mate).wait_send()

    def copy_of(node, way, source, target, device):
        return pltpu.make_async_remote_copy(
            src_ref=source, dst_ref=target, send_sem=piv_send.at[node, way],
            recv_sem=piv_recv.at[node, way], device_id=device, device_id_type=MESH)

    def core_copy(node):
        return copy_of(node, 0, cand.at[node, 1 - core], core_in.at[node], mate)

    def chip_copy(node, d):
        return copy_of(node, 2 + d, chip_sum.at[node], row_in.at[node, d], far[d])

    def sol_copy(node, which):
        return copy_of(node, 1, sol.at[node, which], sol.at[node, which], mate)

    def offer(node, front):
        for c in range(2):
            for h in range(2):
                total = jnp.zeros((depth, half), F32)
                for b in range(per_device):
                    mine = block_ref[node] == row * per_device + b
                    total = jnp.where(
                        mine, front[c, b * depth:(b + 1) * depth, h * half:(h + 1) * half], total)
                cand[node, h, c] = total
        core_copy(node).start()

    def offer_chip(node):
        core_copy(node).wait_recv()
        chip_sum[node] = cand[node, core] + core_in[node]
        for d in range(ny - 1):
            chip_copy(node, d).start()

    def solve(node):
        for d in range(ny - 1):
            chip_copy(node, d).wait_recv()
        pivot = [chip_sum[node, c] for c in range(2)]
        for d in range(ny - 1):
            pivot = [pivot[c] + row_in[node, d, c] for c in range(2)]
        b_high, b_low = halves(jnp.concatenate(pivot, axis=1))
        for first in range(0, depth, TILE):
            rows = slice(first, first + TILE)
            real, imag = [
                mm3(jnp.concatenate([inv[node, c, q, rows, :] for q in range(n_row)], axis=1),
                    b_high, b_low) for c in range(2)]
            sol[node, core, 0, rows, :] = real[:, :half] - imag[:, half:]
            sol[node, core, 1, rows, :] = real[:, half:] + imag[:, :half]
        sol_copy(node, core).start()
        sol_copy(node, 1 - core).wait_recv()
        for c in range(2):
            for h in range(2):
                high, low = halves(sol[node, h, c])
                lanes = slice(c * 2 * half + h * half, c * 2 * half + (h + 1) * half)
                other = slice((1 - c) * 2 * half + h * half, (1 - c) * 2 * half + (h + 1) * half)
                w_high[:depth, lanes] = high
                w_low[:depth, lanes] = low
                w_high[depth:, other] = -high if c == 1 else high
                w_low[depth:, other] = -low if c == 1 else low

    def project(node, first, last):
        @pl.loop(first, last)
        def _(i):
            rows = pl.ds(pl.multiple_of(i * TILE, TILE), TILE)
            factor = jnp.concatenate([pan[node, 0, rows, :], pan[node, 1, rows, :]], axis=1)
            high, low = halves(mm3(factor, w_high[...], w_low[...]))
            u_high[rows, :] = high
            u_low[rows, :] = low

    def apply(node, front):
        @pl.loop(0, front_ref.shape[1] // TILE)
        def _(i):
            start = pl.multiple_of(i * TILE, TILE)
            rows = pl.ds(start, TILE)
            places = start + lax.broadcasted_iota(jnp.int32, (TILE, slots), 0)
            chosen = jnp.where(places == slots_ref[node:node + 1, :], 1.0, 0.0).astype(BF16)
            change = mm(chosen, u_high[...]) + mm(chosen, u_low[...])
            mine = block_ref[node] == row * per_device + start // depth
            inner = pl.ds(pl.multiple_of(start % depth, TILE), TILE)
            for c in range(2):
                for h in range(2):
                    lanes = slice(h * half, (h + 1) * half)
                    base = jnp.where(mine, sol[node, h, c, inner, :], front[c, rows, lanes])
                    first = c * 2 * half + h * half
                    out_ref[c, rows, lanes] = base - change[:, first:first + half]

    own_sends(0)
    own_sends(1)
    offer(0, front_ref)
    steps(0, 1, nz)
    across_wait(0)
    inv_start(0)
    offer_chip(0)
    steps(1, 1, nz)
    for node in range(nodes):
        front = front_ref if node == 0 else out_ref
        inv_relay(node)
        inv_finish(node)
        if node + 1 < nodes:
            own_sends(node + 2)
            inv_start(node + 1)
        solve(node)
        across_wait(node + 1)
        project(node, 0, slots // TILE)
        apply(node, front)
        if node + 1 < nodes:
            offer(node + 1, out_ref)
            steps(node + 2, 1, 2)
            offer_chip(node + 1)
            steps(node + 2, 2, nz)

    for unit in range(nodes + 1):
        sends_wait(unit)
    for node in range(nodes):
        inv_sends_wait(node)
        core_copy(node).wait_send()
        sol_copy(node, core).wait_send()
        for d in range(ny - 1):
            chip_copy(node, d).wait_send()


def solution(mesh):
    n_src, n_row = mesh.shape["src"], mesh.shape["row"]

    def local(right_side, pivot_inverse, ancestor_panel, ancestors, pivot_block):
        nodes, _, shard, depth = ancestor_panel.shape
        slots = shard * n_src
        inv_rows = pivot_inverse.shape[2] * n_src
        columns = right_side.shape[2]
        half, quarter = columns // 2, depth // n_row
        nz, ny = n_src // 2, n_row // 2
        dma = pltpu.SemaphoreType.DMA
        vmem = pl.BlockSpec(memory_space=pltpu.VMEM)
        anywhere = pl.BlockSpec(memory_space=pl.ANY)
        return pl.pallas_call(
            functools.partial(kernel, n_src, n_row),
            out_shape=jax.ShapeDtypeStruct(right_side.shape, F32),
            in_specs=[vmem, anywhere, anywhere, vmem, pl.BlockSpec(memory_space=pltpu.SMEM)],
            out_specs=vmem,
            scratch_shapes=[
                pltpu.VMEM((nodes, 2, slots, depth), F32),
                pltpu.VMEM((nodes, 2, n_row, inv_rows, quarter), F32),
                pltpu.VMEM((nodes, 2, 2, depth, half), F32),
                pltpu.VMEM((nodes, 2, depth, half), F32),
                pltpu.VMEM((nodes, 2, depth, half), F32),
                pltpu.VMEM((nodes, ny - 1, 2, depth, half), F32),
                pltpu.VMEM((nodes, 2, 2, depth, half), F32),
                pltpu.VMEM((2 * depth, 2 * columns), BF16),
                pltpu.VMEM((2 * depth, 2 * columns), BF16),
                pltpu.VMEM((slots, 2 * columns), BF16),
                pltpu.VMEM((slots, 2 * columns), BF16),
                dma((nodes + 1,)),
                dma((nodes + 1, 3, nz)),
                dma((nodes + 1, n_src)),
                dma((nodes, 2 * ny)),
                dma((nodes, n_row)),
                dma((nodes, ny + 1)),
                dma((nodes, ny + 1)),
            ],
            compiler_params=pltpu.CompilerParams(
                collective_id=0, has_side_effects=True, vmem_limit_bytes=56 * 1024 * 1024),
        )(right_side, pivot_inverse, ancestor_panel, ancestors, pivot_block)

    in_specs = (
        P(None, "row", "src"),
        P(None, None, "src", None),
        P(None, None, ("row", "src"), None),
        P(None, "row"),
        P(),
    )
    out_specs = P(None, "row", "src")
    return jax.shard_map(local, mesh=mesh, in_specs=in_specs, out_specs=out_specs, check_vma=False)
```

```python
import functools

import jax
import jax.numpy as jnp
from jax import lax
from jax.experimental import pallas as pl
from jax.experimental.pallas import tpu as pltpu
from jax.sharding import PartitionSpec as P

MESH = pl.DeviceIdType.MESH
F32, BF16 = jnp.float32, jnp.bfloat16
TILE = 256


def halves(value):
    high = value.astype(BF16)
    return high, (value - high.astype(F32)).astype(BF16)


def mm(a, b):
    return jnp.dot(a, b, preferred_element_type=F32)


def mm3(a, b_high, b_low):
    high, low = halves(a)
    return mm(high, b_high) + (mm(high, b_low) + mm(low, b_high))


def kernel(n_src, n_row, front_ref, inverse_ref, panel_ref, slots_ref, block_ref, out_ref,
           pan, inv, cand, core_in, chip_sum, row_in, sol, w_high, w_low, u_high, u_low,
           local_sem, hop_send, hop_recv, inv_send, inv_recv, piv_send, piv_recv):
    nodes, _, shard, depth = panel_ref.shape
    inv_rows = inverse_ref.shape[2]
    quarter = depth // n_row
    half = front_ref.shape[2] // 2
    per_device = front_ref.shape[1] // depth
    slots = slots_ref.shape[1]
    nz, ny = n_src // 2, n_row // 2

    src, row = lax.axis_index("src"), lax.axis_index("row")
    z, x = src // 2, src % 2
    y, core = row // 2, row % 2
    up = {"src": src + 2, "row": row}
    down = {"src": src - 2, "row": row}
    across = {"src": z * 2 + (1 - x), "row": row}
    mate = {"src": src, "row": y * 2 + (1 - core)}
    far = [{"src": src, "row": (y + d) % ny * 2 + core} for d in range(1, ny)]

    def place(unit, jz, jx, part=slice(None)):
        if unit == 0:
            rows = pl.ds(pl.multiple_of((jz * 2 + jx) * inv_rows, 8), inv_rows)
            return inv.at[:, part, row, rows, :]
        return pan.at[unit - 1, part, jx, pl.ds(pl.multiple_of(jz * shard, 8), shard), :]

    own = [pltpu.make_async_copy(
        inverse_ref.at[:, :, :, pl.ds(pl.multiple_of(row * quarter, 128), quarter)],
        place(0, z, x), local_sem.at[0])]
    own += [pltpu.make_async_copy(panel_ref.at[k], place(k + 1, z, x), local_sem.at[k + 1])
            for k in range(nodes)]
    for copy in own:
        copy.start()

    barrier = pltpu.get_barrier_semaphore()

    def greet(device):
        pl.semaphore_signal(barrier, inc=1, device_id=device, device_id_type=MESH)

    @pl.when(z + 1 < nz)
    def _():
        greet(up)

    @pl.when(z > 0)
    def _():
        greet(down)

    for device in [across, mate] + far:
        greet(device)

    ends = jnp.where(z + 1 < nz, 1, 0) + jnp.where(z > 0, 1, 0)
    pl.semaphore_wait(barrier, 2 + len(far) + ends)

    pair = z + 1 - 2 * (z % 2)
    pair_device = {"src": pair * 2 + x, "row": row}

    def hop(unit, jz, jx, way, device, part=slice(None)):
        ref = place(unit, jz, jx, part)
        return pltpu.make_async_remote_copy(
            src_ref=ref, dst_ref=ref, send_sem=hop_send.at[unit, way, jz],
            recv_sem=hop_recv.at[unit, jz * 2 + jx], device_id=device, device_id_type=MESH)

    def extra_hop(unit, jz):
        ref = place(unit, jz, 1 - x, 1)
        return pltpu.make_async_remote_copy(
            src_ref=ref, dst_ref=ref, send_sem=hop_send.at[unit, 3, 0],
            recv_sem=hop_recv.at[unit, n_src], device_id=pair_device, device_id_type=MESH)

    def go_up(unit, jz):
        @pl.when(z + 1 < nz)
        def _():
            hop(unit, jz, x, 0, up).start()

    def go_down(unit, jz):
        @pl.when(z > 0)
        def _():
            hop(unit, jz, x, 1, down).start()

    def go_across(unit, jz):
        @pl.when(jz == pair)
        def _():
            hop(unit, jz, x, 2, across, 0).start()

        @pl.when(jz != pair)
        def _():
            hop(unit, jz, x, 2, across).start()

    def extra(unit):
        hop(unit, z, 1 - x, 2, across).wait_recv()
        extra_hop(unit, z).start()

    def own_sends(unit):
        own[unit].wait()
        go_up(unit, z)
        go_down(unit, z)
        go_across(unit, z)

    def step(unit, t):
        below, above = z - t, z + t

        @pl.when(below >= 0)
        def _():
            hop(unit, below, x, 2, across).wait_recv()
            go_up(unit, below)
            go_across(unit, below)

        @pl.when(above < nz)
        def _():
            hop(unit, above, x, 2, across).wait_recv()
            go_down(unit, above)
            go_across(unit, above)

    def steps(unit, first, last):
        @pl.loop(first, last)
        def _(t):
            step(unit, t)

    def across_wait(unit):
        @pl.loop(0, nz)
        def _(j):
            @pl.when((j != z) & (j != pair))
            def _():
                hop(unit, j, 1 - x, 2, across).wait_recv()

        hop(unit, pair, 1 - x, 2, across, 0).wait_recv()
        extra_hop(unit, pair).wait_recv()

    def sends_wait(unit):
        @pl.loop(0, nz)
        def _(j):
            @pl.when((j <= z) & (z + 1 < nz))
            def _():
                hop(unit, j, x, 0, up).wait_send()

            @pl.when((j >= z) & (z > 0))
            def _():
                hop(unit, j, x, 1, down).wait_send()

            @pl.when(j != pair)
            def _():
                hop(unit, j, x, 2, across).wait_send()

        hop(unit, pair, x, 2, across, 0).wait_send()
        extra_hop(unit, z).wait_send()

    def inv_copy(node, owner_y, owner_core, way, device):
        owner = owner_y * 2 + owner_core
        ref = inv.at[node, :, owner]
        return pltpu.make_async_remote_copy(
            src_ref=ref, dst_ref=ref, send_sem=inv_send.at[node, way],
            recv_sem=inv_recv.at[node, owner], device_id=device, device_id_type=MESH)

    def inv_start(node):
        for d, device in enumerate(far):
            inv_copy(node, y, core, ny + d, device).start()
        inv_copy(node, y, core, 0, mate).start()

    def inv_relay(node):
        for d in range(1, ny):
            other = (y + d) % ny
            inv_copy(node, other, core, 0, mate).wait_recv()
            inv_copy(node, other, core, d, mate).start()

    def inv_finish(node):
        for d in range(ny):
            inv_copy(node, (y + d) % ny, 1 - core, 0, mate).wait_recv()

    def inv_sends_wait(node):
        for d, device in enumerate(far):
            inv_copy(node, y, core, ny + d, device).wait_send()
        for d in range(ny):
            inv_copy(node, (y + d) % ny, core, d, mate).wait_send()

    def copy_of(node, way, source, target, device):
        return pltpu.make_async_remote_copy(
            src_ref=source, dst_ref=target, send_sem=piv_send.at[node, way],
            recv_sem=piv_recv.at[node, way], device_id=device, device_id_type=MESH)

    def core_copy(node):
        return copy_of(node, 0, cand.at[node, 1 - core], core_in.at[node], mate)

    def chip_copy(node, d):
        return copy_of(node, 2 + d, chip_sum.at[node], row_in.at[node, d], far[d])

    def sol_copy(node, which):
        return copy_of(node, 1, sol.at[node, which], sol.at[node, which], mate)

    def offer(node, front):
        for c in range(2):
            for h in range(2):
                total = jnp.zeros((depth, half), F32)
                for b in range(per_device):
                    mine = block_ref[node] == row * per_device + b
                    total = jnp.where(
                        mine, front[c, b * depth:(b + 1) * depth, h * half:(h + 1) * half], total)
                cand[node, h, c] = total
        core_copy(node).start()

    def offer_chip(node):
        core_copy(node).wait_recv()
        chip_sum[node] = cand[node, core] + core_in[node]
        for d in range(ny - 1):
            chip_copy(node, d).start()

    def solve(node):
        for d in range(ny - 1):
            chip_copy(node, d).wait_recv()
        pivot = [chip_sum[node, c] for c in range(2)]
        for d in range(ny - 1):
            pivot = [pivot[c] + row_in[node, d, c] for c in range(2)]
        b_high, b_low = halves(jnp.concatenate(pivot, axis=1))
        for first in range(0, depth, TILE):
            rows = slice(first, first + TILE)
            real, imag = [
                mm3(jnp.concatenate([inv[node, c, q, rows, :] for q in range(n_row)], axis=1),
                    b_high, b_low) for c in range(2)]
            sol[node, core, 0, rows, :] = real[:, :half] - imag[:, half:]
            sol[node, core, 1, rows, :] = real[:, half:] + imag[:, :half]
        sol_copy(node, core).start()
        sol_copy(node, 1 - core).wait_recv()
        for c in range(2):
            for h in range(2):
                high, low = halves(sol[node, h, c])
                lanes = slice(c * 2 * half + h * half, c * 2 * half + (h + 1) * half)
                other = slice((1 - c) * 2 * half + h * half, (1 - c) * 2 * half + (h + 1) * half)
                w_high[:depth, lanes] = high
                w_low[:depth, lanes] = low
                w_high[depth:, other] = -high if c == 1 else high
                w_low[depth:, other] = -low if c == 1 else low

    def project(node, column):
        @pl.loop(0, slots // 2 // TILE)
        def _(i):
            rows = pl.ds(pl.multiple_of(i * TILE, TILE), TILE)
            factor = jnp.concatenate([pan[node, c, column, rows, :] for c in range(2)], axis=1)
            high, low = halves(mm3(factor, w_high[...], w_low[...]))
            for g in range(TILE // shard):
                first = ((i * (TILE // shard) + g) * 2 + column) * shard
                target = pl.ds(pl.multiple_of(first, 16), shard)
                u_high[target, :] = high[g * shard:(g + 1) * shard]
                u_low[target, :] = low[g * shard:(g + 1) * shard]

    def apply(node, front):
        @pl.loop(0, front_ref.shape[1] // TILE)
        def _(i):
            start = pl.multiple_of(i * TILE, TILE)
            rows = pl.ds(start, TILE)
            places = start + lax.broadcasted_iota(jnp.int32, (TILE, slots), 0)
            chosen = jnp.where(places == slots_ref[node:node + 1, :], 1.0, 0.0).astype(BF16)
            change = mm(chosen, u_high[...]) + mm(chosen, u_low[...])
            mine = block_ref[node] == row * per_device + start // depth
            inner = pl.ds(pl.multiple_of(start % depth, TILE), TILE)
            for c in range(2):
                for h in range(2):
                    lanes = slice(h * half, (h + 1) * half)
                    base = jnp.where(mine, sol[node, h, c, inner, :], front[c, rows, lanes])
                    first = c * 2 * half + h * half
                    out_ref[c, rows, lanes] = base - change[:, first:first + half]

    own_sends(0)
    own_sends(1)
    offer(0, front_ref)
    steps(0, 1, nz)
    extra(0)
    across_wait(0)
    inv_start(0)
    offer_chip(0)
    steps(1, 1, nz)
    extra(1)
    inv_relay(0)
    for node in range(nodes):
        front = front_ref if node == 0 else out_ref
        more = node + 1 < nodes
        inv_finish(node)
        if more:
            own_sends(node + 2)
            inv_start(node + 1)
        solve(node)
        project(node, x)
        across_wait(node + 1)
        if more:
            steps(node + 2, 1, 2)
        project(node, 1 - x)
        apply(node, front)
        if more:
            offer(node + 1, out_ref)
            inv_relay(node + 1)
            offer_chip(node + 1)
            steps(node + 2, 2, nz)
            extra(node + 2)

    for unit in range(nodes + 1):
        sends_wait(unit)
    for node in range(nodes):
        inv_sends_wait(node)
        core_copy(node).wait_send()
        sol_copy(node, core).wait_send()
        for d in range(ny - 1):
            chip_copy(node, d).wait_send()


def solution(mesh):
    n_src, n_row = mesh.shape["src"], mesh.shape["row"]

    def local(right_side, pivot_inverse, ancestor_panel, ancestors, pivot_block):
        nodes, _, shard, depth = ancestor_panel.shape
        slots = shard * n_src
        inv_rows = pivot_inverse.shape[2] * n_src
        columns = right_side.shape[2]
        half, quarter = columns // 2, depth // n_row
        nz, ny = n_src // 2, n_row // 2
        dma = pltpu.SemaphoreType.DMA
        vmem = pl.BlockSpec(memory_space=pltpu.VMEM)
        anywhere = pl.BlockSpec(memory_space=pl.ANY)
        return pl.pallas_call(
            functools.partial(kernel, n_src, n_row),
            out_shape=jax.ShapeDtypeStruct(right_side.shape, F32),
            in_specs=[vmem, anywhere, anywhere, vmem, pl.BlockSpec(memory_space=pltpu.SMEM)],
            out_specs=vmem,
            scratch_shapes=[
                pltpu.VMEM((nodes, 2, 2, slots // 2, depth), F32),
                pltpu.VMEM((nodes, 2, n_row, inv_rows, quarter), F32),
                pltpu.VMEM((nodes, 2, 2, depth, half), F32),
                pltpu.VMEM((nodes, 2, depth, half), F32),
                pltpu.VMEM((nodes, 2, depth, half), F32),
                pltpu.VMEM((nodes, ny - 1, 2, depth, half), F32),
                pltpu.VMEM((nodes, 2, 2, depth, half), F32),
                pltpu.VMEM((2 * depth, 2 * columns), BF16),
                pltpu.VMEM((2 * depth, 2 * columns), BF16),
                pltpu.VMEM((slots, 2 * columns), BF16),
                pltpu.VMEM((slots, 2 * columns), BF16),
                dma((nodes + 1,)),
                dma((nodes + 1, 4, nz)),
                dma((nodes + 1, n_src + 1)),
                dma((nodes, 2 * ny)),
                dma((nodes, n_row)),
                dma((nodes, ny + 1)),
                dma((nodes, ny + 1)),
            ],
            compiler_params=pltpu.CompilerParams(
                collective_id=0, has_side_effects=True, vmem_limit_bytes=56 * 1024 * 1024),
        )(right_side, pivot_inverse, ancestor_panel, ancestors, pivot_block)

    in_specs = (
        P(None, "row", "src"),
        P(None, None, "src", None),
        P(None, None, ("row", "src"), None),
        P(None, "row"),
        P(),
    )
    out_specs = P(None, "row", "src")
    return jax.shard_map(local, mesh=mesh, in_specs=in_specs, out_specs=out_specs, check_vma=False)
```
